32 devices in a mesh: row: 8 (over y, x, core), col: 4 (over z).
Axes of the slice: x: 2, y: 2, z: 4, core: 2. Of those that a mesh axis runs over, the one named last changes fastest.
Arguments:
- harmonic: int32 [4, 1024], P('col', 'row'), may hold values from 0 to 312, as said below
- legendre: float32 [2, 4, 1024, 512], P(None, 'col', 'row'), may hold values from -6 to 6
- whitening: float32 [2, 512, 512], replicated
- longitude: float32 [2, 512], replicated, may hold values from -3.140625 to 3.140625
- observed: float32 [2, 512], replicated, may hold values from -6 to 6
Outputs:
- normal: float32 [4096, 4096], P('row', 'col')
- rhs: float32 [4, 1024], P('col', 'row')
The draws below stay inside these ranges and needn't reach their ends.
Inputs may be any that keep to these rules, and one draw needn't show every extreme that they name: `harmonic`: A value is m for a cosine column and 156 + m for a sine column (m >= 1); the columns are the first 4095 coefficients of the list ordered by degree up to 156, together with the sine coefficient of degree and order 156, each once, in a random order.
All inputs are finite; a program needn't handle non-finite values.
Results may differ from the reference program's by a relative error of at most 0.00009.
Values sent between devices are 32-bit elements; how exact they have to be, the bound alone decides.
A program may use at most 64 MiB of HBM per device.

```python
import math
import jax
import jax.numpy as jnp
import numpy as np
from jax import lax

LMAX = 156
OBS = 512
ARCS = 2
COLB = 1024
P_SIZE = 4096
N_COL = 4


def draw_harmonic(key, part):
    code_list = []
    for degree in range(LMAX + 1):
        code_list.append(0)
        for order in range(1, degree + 1):
            code_list.append(order)
            code_list.append(LMAX + order)
    chosen = code_list[:P_SIZE - 1] + [2 * LMAX]
    table = jnp.asarray(np.array(chosen, dtype=np.int32))
    shuffle = jax.random.permutation(jax.random.fold_in(key, 11), P_SIZE)
    return table[shuffle].reshape(N_COL, COLB).astype(jnp.int32)


def draw_whitening(key, part):
    first_key, second_key = jax.random.split(jax.random.fold_in(key, 23), 2)
    diagonal = jax.random.uniform(first_key, (ARCS, OBS), jnp.float32, 0.5, 1.5)
    off_diag = jax.random.normal(second_key, (ARCS, OBS, OBS), jnp.float32) * (0.5 / math.sqrt(OBS))
    identity = jnp.eye(OBS, dtype=jnp.float32)
    matrix = off_diag + diagonal[:, :, None] * identity[None]
    return (matrix / math.sqrt(OBS)).astype(jnp.float32)


def steps_of(rng, dims, cuts, smallest, largest):
    def one(axis_at, blocks):
        draws = jax.random.uniform(jax.random.fold_in(jax.random.fold_in(rng, 6), axis_at), (blocks,), jnp.float32, smallest / len(cuts), largest / len(cuts))
        return jnp.repeat(jnp.exp(draws), dims[axis_at] // blocks).reshape((-1,) + (1,) * (len(dims) - axis_at - 1))

    factor_of = one(*cuts[0])
    for cut in cuts[1:]:
        factor_of = factor_of * one(*cut)
    return factor_of


def noise(rng, dims, width, most, shards=(), kind=jnp.bfloat16):
    values = jax.random.normal(rng, dims, jnp.float32) * width
    if len(shards) > 0:
        values = steps_of(rng, dims, shards, -0.22, 0.18) * values
    return jnp.clip(values, min=-most, max=most).astype(kind)


def setup_inputs(seed: int = 0) -> dict:
    streams_of = jax.random.split(jax.random.key(seed), 6)
    harmonic = draw_harmonic(jax.random.fold_in(streams_of[5], 71), 0)
    legendre = noise(streams_of[1], (ARCS, N_COL, COLB, OBS), 1.0, 6.0, ((1, 4), (2, 8)), jnp.float32)
    whitening = draw_whitening(jax.random.fold_in(streams_of[5], 71), 0)
    longitude = jnp.clip(jax.random.uniform(streams_of[3], (ARCS, OBS), jnp.float32, -3.140625, 3.140625), -3.140625, 3.140625)
    observed = noise(streams_of[4], (ARCS, OBS), 1.0, 6.0, (), jnp.float32)
    return {"harmonic": harmonic, "legendre": legendre, "whitening": whitening, "longitude": longitude, "observed": observed}


def form_columns(azimuth, leg_values, whitening, longitude):
    is_cosine = azimuth <= LMAX
    orders = jnp.where(is_cosine, azimuth, azimuth - LMAX).astype(jnp.float32)
    phase_angle = orders[None, :, None] * longitude[:, None, :]
    azimuth_terms = jnp.where(is_cosine[None, :, None], jnp.cos(phase_angle), jnp.sin(phase_angle))
    design_t = leg_values * azimuth_terms
    return jnp.einsum("apo,aqo->apq", design_t, whitening, precision=lax.Precision.HIGHEST)


def reference(harmonic, legendre, whitening, longitude, observed):
    azimuth = harmonic.reshape(-1).astype(jnp.int32)
    leg_values = legendre.reshape(ARCS, -1, OBS)
    whitened_t = form_columns(azimuth, leg_values, whitening, longitude)
    white_obs = jnp.einsum("aqo,ao->aq", whitening, observed, precision=lax.Precision.HIGHEST)
    normal = jnp.einsum("aio,ajo->ij", whitened_t, whitened_t, precision=lax.Precision.HIGHEST)
    rhs = jnp.einsum("apq,aq->p", whitened_t, white_obs, precision=lax.Precision.HIGHEST)
    return normal, rhs.reshape(N_COL, COLB)
```

```python
import jax
import jax.numpy as jnp
from jax import lax
from jax.experimental import pallas as pl
from jax.experimental.pallas import tpu as pltpu
from jax.sharding import PartitionSpec as P

LMAX = 156
CHUNKS = 4
MESH = pl.DeviceIdType.MESH


def azimuth_wave(orders, is_sine, longitude):
    angle = orders * longitude
    turns = jnp.floor(angle * 0.6366197723675814 + 0.5)
    rest = angle - turns * 1.5703125
    rest = rest - turns * 4.837512969970703125e-4
    rest = rest - turns * 7.54978995489188216e-8
    sq = rest * rest
    sine = rest + rest * sq * (-1.6666654611e-1 + sq * (8.3321608736e-3 - 1.9515295891e-4 * sq))
    cosine = 1.0 - 0.5 * sq + sq * sq * (
        4.166664568298827e-2 + sq * (-1.388731625493765e-3 + 2.443315711809948e-5 * sq)
    )
    quarter = turns.astype(jnp.int32) - is_sine
    value = jnp.where((quarter & 1) == 1, sine, cosine)
    return jnp.where(((quarter + 1) & 2) == 2, -value, value)


def split(value):
    high = value.astype(jnp.bfloat16)
    return high, (value - high.astype(jnp.float32)).astype(jnp.bfloat16)


def dot_t(a, b):
    return lax.dot_general(a, b, (((1,), (1,)), ((), ())), preferred_element_type=jnp.float32)


def dot3(a_high, a_low, b_high, b_low):
    return dot_t(a_high, b_low) + dot_t(a_low, b_high) + dot_t(a_high, b_high)


def kernel(
    planes,
    harmonic_ref, leg_ref, whitening_ref, longitude_ref, observed_ref,
    normal_ref, rhs_ref,
    cols, rows, col_high, col_low, row_high, row_low,
    s_x, s_y, s_d, s_c, s_up, s_dn,
    r_x, r_y, r_d, r_c, r_z,
):
    arcs, width, obs = leg_ref.shape
    per_arc = CHUNKS // arcs
    me = lax.axis_index("row")
    z = lax.axis_index("col")
    y, x, core = me // 4, (me // 2) % 2, me % 2
    chip = me // 2

    def at(yy, xx, cc):
        return 4 * yy + 2 * xx + cc

    near_x = at(y, 1 - x, core)
    near_y = at(1 - y, x, core)
    across = at(1 - y, 1 - x, core)
    twin = at(y, x, 1 - core)
    mine = (me, near_x, near_y, across)
    other = (twin, at(y, 1 - x, 1 - core), at(1 - y, x, 1 - core), at(1 - y, 1 - x, 1 - core))
    low_z, high_z = jnp.maximum(z - 1, 0), jnp.minimum(z + 1, planes - 1)

    barrier = pltpu.get_barrier_semaphore()
    for peer in (near_x, near_y, twin):
        pl.semaphore_signal(barrier, inc=1, device_id={"row": peer}, device_id_type=MESH)

    @pl.when(z > 0)
    def _():
        pl.semaphore_signal(barrier, inc=1, device_id={"col": low_z}, device_id_type=MESH)

    @pl.when(z < planes - 1)
    def _():
        pl.semaphore_signal(barrier, inc=1, device_id={"col": high_z}, device_id_type=MESH)

    code = jnp.transpose(jnp.broadcast_to(harmonic_ref[...], (width, width)))[:, :1]
    is_sine = jnp.where(code > LMAX, 1, 0)
    orders = (code - LMAX * is_sine).astype(jnp.float32)
    rows_per = width // per_arc
    rhs = jnp.zeros((8, width), jnp.float32)
    for a in range(arcs):
        wave = azimuth_wave(orders, is_sine, longitude_ref[a : a + 1, :])
        d_high, d_low = split(leg_ref[a] * wave)
        w_high, w_low = split(whitening_ref[a])
        part = dot3(d_high, d_low, w_high, w_low)
        for i in range(per_arc):
            cols[me, a * per_arc + i] = part[i * rows_per : (i + 1) * rows_per]
        o_high, o_low = split(jnp.broadcast_to(observed_ref[a : a + 1, :], (8, obs)))
        g_high, g_low = split(dot3(o_high, o_low, w_high, w_low))
        p_high, p_low = split(part)
        rhs = rhs + dot3(g_high, g_low, p_high, p_low)
    rhs_ref[...] = rhs[:1]

    inner = jnp.where(z > 0, 1, 0) + jnp.where(z < planes - 1, 1, 0)
    pl.semaphore_wait(barrier, 3 + inner)

    def copy(src, dst, s, r, **device):
        return pltpu.make_async_remote_copy(
            src_ref=src, dst_ref=dst, send_sem=s, recv_sem=r, device_id=device, device_id_type=MESH
        )

    def block(slot, c):
        return cols.at[slot, c]

    def to_x(c):
        return copy(block(me, c), block(me, c), s_x.at[c], r_x.at[c], row=near_x)

    def to_y(c):
        return copy(block(me, c), block(me, c), s_y.at[c], r_y.at[c], row=near_y)

    def to_across(c):
        if c < CHUNKS // 2:
            return copy(block(near_x, c), block(near_x, c), s_d.at[c], r_d.at[c], row=near_y)
        return copy(block(near_y, c), block(near_y, c), s_d.at[c], r_d.at[c], row=near_x)

    def to_twin(j, c):
        return copy(block(mine[j], c), block(mine[j], c), s_c.at[j, c], r_c.at[j, c], row=twin)

    def wait_x(c):
        copy(block(near_x, c), block(near_x, c), s_x.at[c], r_x.at[c], row=near_x).wait_recv()

    def wait_y(c):
        copy(block(near_y, c), block(near_y, c), s_y.at[c], r_y.at[c], row=near_y).wait_recv()

    def wait_across(c):
        copy(block(across, c), block(across, c), s_d.at[c], r_d.at[c], row=near_x).wait_recv()

    def wait_twin(j, c):
        copy(block(other[j], c), block(other[j], c), s_c.at[j, c], r_c.at[j, c], row=twin).wait_recv()

    source = z == chip
    own_half = y == core
    goes_up = (z >= chip) & (z < planes - 1)
    goes_down = (z <= chip) & (z > 0)
    far_y = y + core - 2 * y * core
    line_y = y + far_y - 2 * y * far_y

    def line_slot(q):
        xx = x if q < 2 else 1 - x
        cc = core if q % 2 == 0 else 1 - core
        return at(line_y, xx, cc)

    def up(src, q, c):
        return copy(src, rows.at[q, c], s_up.at[q, c], r_z.at[q, c], col=high_z)

    def down(src, q, c):
        return copy(src, rows.at[q, c], s_dn.at[q, c], r_z.at[q, c], col=low_z)

    def send_line(src, q, c):
        @pl.when(goes_up)
        def _():
            up(src, q, c).start()

        @pl.when(goes_down)
        def _():
            down(src, q, c).start()

    def from_source(condition, q, c):
        @pl.when(source & condition)
        def _():
            send_line(block(line_slot(q), c), q, c)

    def pass_on(q, c):
        @pl.when(jnp.logical_not(source))
        def _():
            copy(rows.at[q, c], rows.at[q, c], s_up.at[q, c], r_z.at[q, c], col=low_z).wait_recv()
            send_line(rows.at[q, c], q, c)

    far_half = jnp.logical_not(own_half)
    stream = [(2 * h + i, c) for h in range(2) for c in range(CHUNKS) for i in range(2)]
    per_tile = width * 2

    def convert_cols(slot):
        for c in range(CHUNKS):
            a, i = c // per_arc, c % per_arc
            high, low = split(cols[slot, c])
            start = pl.multiple_of(slot * width + i * rows_per, rows_per)
            col_high[pl.ds(start, rows_per), pl.ds(a * obs, obs)] = high
            col_low[pl.ds(start, rows_per), pl.ds(a * obs, obs)] = low

    def convert_rows(half):
        def put(q, c, value):
            a, i = c // per_arc, c % per_arc
            high, low = split(value)
            start = (line_slot(q) % 2) * width + i * rows_per
            start = pl.multiple_of(start, rows_per)
            row_high[pl.ds(start, rows_per), pl.ds(a * obs, obs)] = high
            row_low[pl.ds(start, rows_per), pl.ds(a * obs, obs)] = low

        @pl.when(source)
        def _():
            for q in (2 * half, 2 * half + 1):
                for c in range(CHUNKS):
                    put(q, c, cols[line_slot(q), c])

        @pl.when(jnp.logical_not(source))
        def _():
            for q in (2 * half, 2 * half + 1):
                for c in range(CHUNKS):
                    put(q, c, rows[q, c])

    def multiply(half):
        xx = x if half == 0 else 1 - x
        top = pl.multiple_of(xx * per_tile, per_tile)

        def one(j, carry):
            left = pl.multiple_of(j * per_tile, per_tile)
            normal_ref[pl.ds(top, per_tile), pl.ds(left, per_tile)] = dot3(
                row_high[...], row_low[...],
                col_high[pl.ds(left, per_tile), :], col_low[pl.ds(left, per_tile), :],
            )
            return carry

        lax.fori_loop(0, col_high.shape[0] // per_tile, one, 0)

    for c in range(CHUNKS):
        to_x(c).start()
        to_y(c).start()
        to_twin(0, c).start()
        from_source(own_half, 0, c)
    for c in range(CHUNKS):
        wait_twin(0, c)
        from_source(own_half, 1, c)
    convert_cols(me)
    convert_cols(twin)
    done = 0
    for c in range(CHUNKS):
        wait_x(c)
        if c < CHUNKS // 2:
            to_across(c).start()
        to_twin(1, c).start()
        from_source(own_half, 2, c)
        wait_y(c)
        if c >= CHUNKS // 2:
            to_across(c).start()
        to_twin(2, c).start()
        from_source(far_half, 0, c)
        wait_twin(1, c)
        from_source(own_half, 3, c)
        wait_twin(2, c)
        from_source(far_half, 1, c)
        if c > 0:
            pass_on(*stream[done])
            done += 1
    for c in range(CHUNKS):
        wait_across(c)
        to_twin(3, c).start()
        from_source(far_half, 2, c)
        wait_twin(3, c)
        from_source(far_half, 3, c)
        pass_on(*stream[done])
        done += 1
    for slot in (mine[1], mine[2], mine[3], other[1], other[2], other[3]):
        convert_cols(slot)
    while done < 2 * CHUNKS:
        pass_on(*stream[done])
        done += 1
    convert_rows(0)
    multiply(0)
    while done < 4 * CHUNKS:
        pass_on(*stream[done])
        done += 1
    convert_rows(1)
    multiply(1)

    for c in range(CHUNKS):
        to_x(c).wait_send()
        to_y(c).wait_send()
        to_across(c).wait_send()
        for j in range(4):
            to_twin(j, c).wait_send()

    @pl.when(goes_up)
    def _():
        for q, c in stream:
            up(rows.at[q, c], q, c).wait_send()

    @pl.when(goes_down)
    def _():
        for q, c in stream:
            down(rows.at[q, c], q, c).wait_send()


def fused(row_count, planes):
    def body(harmonic, legendre, whitening, longitude, observed):
        arcs, _, width, obs = legendre.shape
        depth = arcs * obs
        tall = row_count * width
        chunk_rows = arcs * width // CHUNKS
        dma = pltpu.SemaphoreType.DMA
        vmem = pl.BlockSpec(memory_space=pltpu.VMEM)
        normal, rhs = pl.pallas_call(
            lambda *refs: kernel(planes, *refs),
            out_shape=(
                jax.ShapeDtypeStruct((planes * width, tall), jnp.float32),
                jax.ShapeDtypeStruct((1, width), jnp.float32),
            ),
            in_specs=[vmem] * 5,
            out_specs=(vmem, vmem),
            scratch_shapes=[
                pltpu.VMEM((row_count, CHUNKS, chunk_rows, obs), jnp.float32),
                pltpu.VMEM((4, CHUNKS, chunk_rows, obs), jnp.float32),
                pltpu.VMEM((tall, depth), jnp.bfloat16),
                pltpu.VMEM((tall, depth), jnp.bfloat16),
                pltpu.VMEM((2 * width, depth), jnp.bfloat16),
                pltpu.VMEM((2 * width, depth), jnp.bfloat16),
                dma((CHUNKS,)), dma((CHUNKS,)), dma((CHUNKS,)), dma((4, CHUNKS)),
                dma((4, CHUNKS)), dma((4, CHUNKS)),
                dma((CHUNKS,)), dma((CHUNKS,)), dma((CHUNKS,)), dma((4, CHUNKS)),
                dma((4, CHUNKS)),
            ],
            compiler_params=pltpu.CompilerParams(
                collective_id=0, has_side_effects=True, vmem_limit_bytes=48 * 1024 * 1024
            ),
            name="normal_tile",
        )(harmonic, legendre.reshape(arcs, width, obs), whitening, longitude, observed)
        return normal, rhs

    return body


def general(harmonic, legendre, whitening, longitude, observed):
    arcs = legendre.shape[0]
    azimuth = harmonic.reshape(-1)
    leg = legendre.reshape(arcs, -1, legendre.shape[3])
    is_sine = jnp.where(azimuth > LMAX, 1, 0)
    orders = (azimuth - LMAX * is_sine).astype(jnp.float32)
    wave = azimuth_wave(orders[None, :, None], is_sine[None, :, None], longitude[:, None, :])
    high = lax.Precision.HIGH
    portion = jnp.einsum("apo,aqo->apq", leg * wave, whitening, precision=high)
    white_obs = jnp.einsum("aqo,ao->aq", whitening, observed, precision=high)
    rhs = jnp.einsum("apq,aq->p", portion, white_obs, precision=high).reshape(1, -1)
    row_width = portion.shape[1] * lax.axis_size("col")
    groups = lax.axis_size("row") // lax.axis_size("col")
    row_index = lax.axis_index("row")
    column_set = lax.all_gather(portion, "row", axis=1, tiled=True)
    own = lax.dynamic_slice_in_dim(column_set, row_index % groups * row_width, row_width, 1)
    kept = jnp.where(lax.axis_index("col") == row_index // groups, own, 0)
    row_set = lax.psum(kept, "col")
    return jnp.einsum("aio,ajo->ij", row_set, column_set, precision=high), rhs


def solution(mesh):
    in_specs = (P("col", "row"), P(None, "col", "row", None), P(), P(), P())
    out_specs = (P("row", "col"), P("col", "row"))
    row_count, planes = mesh.shape["row"], mesh.shape["col"]
    cube = row_count == 2 ** 3 and row_count == 2 * planes
    body = fused(row_count, planes) if cube else general
    return jax.shard_map(body, mesh=mesh, in_specs=in_specs, out_specs=out_specs, check_vma=False)
```

```python
import jax
import jax.numpy as jnp
from jax import lax
from jax.experimental import pallas as pl
from jax.experimental.pallas import tpu as pltpu
from jax.sharding import PartitionSpec as P

LMAX = 156
CHUNKS = 4
MESH = pl.DeviceIdType.MESH


def azimuth_wave(orders, is_sine, longitude):
    angle = orders * longitude
    turns = jnp.floor(angle * 0.6366197723675814 + 0.5)
    rest = angle - turns * 1.5703125
    rest = rest - turns * 4.837512969970703125e-4
    rest = rest - turns * 7.54978995489188216e-8
    sq = rest * rest
    sine = rest + rest * sq * (-1.6666654611e-1 + sq * (8.3321608736e-3 - 1.9515295891e-4 * sq))
    cosine = 1.0 - 0.5 * sq + sq * sq * (
        4.166664568298827e-2 + sq * (-1.388731625493765e-3 + 2.443315711809948e-5 * sq)
    )
    quarter = turns.astype(jnp.int32) - is_sine
    value = jnp.where((quarter & 1) == 1, sine, cosine)
    return jnp.where(((quarter + 1) & 2) == 2, -value, value)


def split(value):
    high = value.astype(jnp.bfloat16)
    return high, (value - high.astype(jnp.float32)).astype(jnp.bfloat16)


def dot_t(a, b):
    return lax.dot_general(a, b, (((1,), (1,)), ((), ())), preferred_element_type=jnp.float32)


def dot3(a_high, a_low, b_high, b_low):
    return dot_t(a_high, b_low) + dot_t(a_low, b_high) + dot_t(a_high, b_high)


def kernel(
    planes,
    harmonic_in, leg_in, whitening_in, longitude_in, observed_in,
    normal_ref, rhs_ref,
    harmonic_ref, leg_ref, whitening_ref, longitude_ref, observed_ref,
    cols, rows, col_high, col_low, row_high, row_low, side, turn,
    s_in, s_x, s_y, s_d, s_c, s_up, s_dn, s_side, s_give, s_turn,
    r_x, r_y, r_d, r_c, r_z, r_side, r_turn,
):
    fetches = [
        pltpu.make_async_copy(src, dst, s_in.at[n])
        for n, (src, dst) in enumerate((
            (harmonic_in, harmonic_ref), (longitude_in, longitude_ref), (observed_in, observed_ref),
            (leg_in, leg_ref), (whitening_in, whitening_ref),
        ))
    ]
    for fetch in fetches:
        fetch.start()
    arcs, width, obs = leg_ref.shape
    per_arc = CHUNKS // arcs
    me = lax.axis_index("row")
    z = lax.axis_index("col")
    y, x, core = me // 4, (me // 2) % 2, me % 2
    chip = me // 2

    def at(yy, xx, cc):
        return 4 * yy + 2 * xx + cc

    near_x = at(y, 1 - x, core)
    near_y = at(1 - y, x, core)
    across = at(1 - y, 1 - x, core)
    twin = at(y, x, 1 - core)
    mine = (me, near_x, near_y, across)
    other = (twin, at(y, 1 - x, 1 - core), at(1 - y, x, 1 - core), at(1 - y, 1 - x, 1 - core))
    low_z, high_z = jnp.maximum(z - 1, 0), jnp.minimum(z + 1, planes - 1)

    barrier = pltpu.get_barrier_semaphore()
    for peer in (near_x, near_y, twin, other[1], other[2]):
        pl.semaphore_signal(barrier, inc=1, device_id={"row": peer}, device_id_type=MESH)

    @pl.when(z > 0)
    def _():
        pl.semaphore_signal(barrier, inc=1, device_id={"col": low_z}, device_id_type=MESH)

    @pl.when(z < planes - 1)
    def _():
        pl.semaphore_signal(barrier, inc=1, device_id={"col": high_z}, device_id_type=MESH)

    for fetch in fetches:
        fetch.wait()
    code = jnp.transpose(jnp.broadcast_to(harmonic_ref[...], (width, width)))[:, :1]
    is_sine = jnp.where(code > LMAX, 1, 0)
    orders = (code - LMAX * is_sine).astype(jnp.float32)
    rows_per = width // per_arc
    rhs = jnp.zeros((8, width), jnp.float32)
    for a in range(arcs):
        wave = azimuth_wave(orders, is_sine, longitude_ref[a : a + 1, :])
        d_high, d_low = split(leg_ref[a] * wave)
        w_high, w_low = split(whitening_ref[a])
        part = dot3(d_high, d_low, w_high, w_low)
        for i in range(per_arc):
            cols[me, a * per_arc + i] = part[i * rows_per : (i + 1) * rows_per]
        o_high, o_low = split(jnp.broadcast_to(observed_ref[a : a + 1, :], (8, obs)))
        g_high, g_low = split(dot3(o_high, o_low, w_high, w_low))
        p_high, p_low = split(part)
        rhs = rhs + dot3(g_high, g_low, p_high, p_low)
    rhs_ref[...] = rhs[:1]

    inner = jnp.where(z > 0, 1, 0) + jnp.where(z < planes - 1, 1, 0)
    pl.semaphore_wait(barrier, 5 + inner)

    def copy(src, dst, s, r, **device):
        return pltpu.make_async_remote_copy(
            src_ref=src, dst_ref=dst, send_sem=s, recv_sem=r, device_id=device, device_id_type=MESH
        )

    def block(slot, c):
        return cols.at[slot, c]

    def to_x(c):
        return copy(block(me, c), block(me, c), s_x.at[c], r_x.at[c], row=near_x)

    def to_y(c):
        return copy(block(me, c), block(me, c), s_y.at[c], r_y.at[c], row=near_y)

    def to_across(c):
        if c < CHUNKS // 2:
            return copy(block(near_x, c), block(near_x, c), s_d.at[c], r_d.at[c], row=near_y)
        return copy(block(near_y, c), block(near_y, c), s_d.at[c], r_d.at[c], row=near_x)

    def to_twin(j, c):
        return copy(block(mine[j], c), block(mine[j], c), s_c.at[j, c], r_c.at[j, c], row=twin)

    def wait_x(c):
        copy(block(near_x, c), block(near_x, c), s_x.at[c], r_x.at[c], row=near_x).wait_recv()

    def wait_y(c):
        copy(block(near_y, c), block(near_y, c), s_y.at[c], r_y.at[c], row=near_y).wait_recv()

    def wait_across(c):
        copy(block(across, c), block(across, c), s_d.at[c], r_d.at[c], row=near_x).wait_recv()

    def wait_twin(j, c):
        copy(block(other[j], c), block(other[j], c), s_c.at[j, c], r_c.at[j, c], row=twin).wait_recv()

    source = z == chip
    own_half = y == core
    goes_up = (z >= chip) & (z < planes - 1)
    goes_down = (z <= chip) & (z > 0)
    far_y = y + core - 2 * y * core
    line_y = y + far_y - 2 * y * far_y

    def line_slot(q):
        xx = x if q < 2 else 1 - x
        cc = core if q % 2 == 0 else 1 - core
        return at(line_y, xx, cc)

    last = planes - 1
    by_side = ((z < chip) & (core == 0)) | ((z > chip) & (core == 1))
    side_x = jnp.where(core == 0, 0, 1)
    swap = jnp.where(by_side & (x == side_x), 1, 0)

    def up(src, q, c):
        return copy(src, rows.at[q, c], s_up.at[q, c], r_z.at[q, c], col=high_z)

    def down(src, q, c):
        return copy(src, rows.at[q, c], s_dn.at[q, c], r_z.at[q, c], col=low_z)

    def rides_up(q):
        has_side_x = (x == side_x) if q < 2 else (x != side_x)
        return source & goes_up & jnp.logical_not(has_side_x & (core == 1))

    def rides_down(q):
        has_side_x = (x == side_x) if q < 2 else (x != side_x)
        return source & goes_down & jnp.logical_not(has_side_x & (core == 0))

    def from_source(condition, q, c):
        @pl.when(condition & rides_up(q))
        def _():
            up(block(line_slot(q), c), q, c).start()

        @pl.when(condition & rides_down(q))
        def _():
            down(block(line_slot(q), c), q, c).start()

    relay = jnp.logical_not(source)

    def place(h):
        return h + swap - 2 * h * swap

    def onward(h):
        return relay if h == 0 else relay & jnp.logical_not(by_side)

    def pass_on(h, i, c):
        q = 2 * place(h) + i

        @pl.when(relay)
        def _():
            up(rows.at[q, c], q, c).wait_recv()

        @pl.when(onward(h) & goes_up)
        def _():
            up(rows.at[q, c], q, c).start()

        @pl.when(onward(h) & goes_down)
        def _():
            down(rows.at[q, c], q, c).start()

    on_side = (chip == 0) | (chip == last)
    level = jnp.where(chip == last, last - z, z)
    further = jnp.where(chip == 0, low_z, high_z)

    def side_send(t, c):
        src = block(me, c) if t == 0 else side.at[t - 1, c]
        return copy(src, side.at[t, c], s_side.at[t, c], r_side.at[t, c], col=further)

    def side_on(t):
        held = on_side & (level > 0)
        return held if t == 0 else held & (level + t <= last)

    def give_x(t, c):
        q = 2 + far_y
        return copy(side.at[t - 1, c], rows.at[q, c], s_give.at[t - 1, c], r_z.at[q, c], row=at(y, 1 - x, y))

    def give_y(t, c):
        q = far_y
        return copy(side.at[t - 1, c], rows.at[q, c], s_give.at[t - 1, c], r_z.at[q, c], row=at(1 - y, x, y))

    def give_turn(t, c):
        peer = near_x if c < CHUNKS // 2 else near_y
        return copy(side.at[t - 1, c], turn.at[c], s_give.at[t - 1, c], r_turn.at[c], row=peer)

    gives = ((1, give_x), (2, give_y), (3, give_turn))

    def side_step(t, c):
        @pl.when(on_side & (level + t <= last))
        def _():
            side_send(t - 1, c).wait_recv()
            if t < last:
                @pl.when(level > 0)
                def _():
                    side_send(t, c).start()
            for k, give in gives:
                if k >= t:
                    @pl.when(level + t == k)
                    def _():
                        give(t, c).start()

    def turn_on(c):
        from_low = (x == 1) if c < CHUNKS // 2 else (x == 0)
        there = (from_low & (z < last)) | (jnp.logical_not(from_low) & (z > 0))
        return jnp.logical_not(on_side) & there

    def turn_send(c):
        if c < CHUNKS // 2:
            q, peer = 2 + far_y, at(1 - y, x, y)
        else:
            q, peer = 3 - far_y, at(y, 1 - x, 1 - y)
        return copy(turn.at[c], rows.at[q, c], s_turn.at[c], r_z.at[q, c], row=peer)

    def turn_step(c):
        @pl.when(turn_on(c))
        def _():
            copy(turn.at[c], turn.at[c], s_turn.at[c], r_turn.at[c], row=near_x).wait_recv()
            turn_send(c).start()

    far_half = jnp.logical_not(own_half)
    stream = [(h, i, c) for h in range(2) for c in range(CHUNKS) for i in range(2)]
    per_tile = width * 2
    tiles = col_high.shape[0] // per_tile

    def convert_cols(slot):
        for c in range(CHUNKS):
            a, i = c // per_arc, c % per_arc
            high, low = split(cols[slot, c])
            start = pl.multiple_of(slot * width + i * rows_per, rows_per)
            col_high[pl.ds(start, rows_per), pl.ds(a * obs, obs)] = high
            col_low[pl.ds(start, rows_per), pl.ds(a * obs, obs)] = low

    def convert_rows(h, a):
        def put(i, c, value):
            high, low = split(value)
            cc = core if i == 0 else 1 - core
            start = pl.multiple_of(cc * width + (c % per_arc) * rows_per, rows_per)
            row_high[h, pl.ds(start, rows_per), pl.ds(a * obs, obs)] = high
            row_low[h, pl.ds(start, rows_per), pl.ds(a * obs, obs)] = low

        for i in range(2):
            for c in range(a * per_arc, (a + 1) * per_arc):
                @pl.when(source)
                def _():
                    put(i, c, cols[line_slot(2 * h + i), c])

                @pl.when(relay)
                def _():
                    put(i, c, rows[2 * place(h) + i, c])

    def multiply(h, start, stop, low_a, high_a, add):
        turned = place(h)
        xx = x + turned - 2 * x * turned
        top = pl.multiple_of(xx * per_tile, per_tile)
        depth = slice(low_a * obs, high_a * obs)

        def one(j, carry):
            left = pl.multiple_of(j * per_tile, per_tile)
            tile = (pl.ds(top, per_tile), pl.ds(left, per_tile))
            part = dot3(
                row_high[h, :, depth], row_low[h, :, depth],
                col_high[pl.ds(left, per_tile), depth], col_low[pl.ds(left, per_tile), depth],
            )
            normal_ref[tile] = normal_ref[tile] + part if add else part
            return carry

        lax.fori_loop(start, stop, one, 0)

    for c in range(CHUNKS):
        @pl.when(side_on(0))
        def _():
            side_send(0, c).start()

        to_x(c).start()
        to_y(c).start()
        to_twin(0, c).start()
        from_source(own_half, 0, c)
    for c in range(CHUNKS):
        wait_twin(0, c)
        from_source(own_half, 1, c)
    convert_cols(me)
    convert_cols(twin)
    done = 0
    for c in range(CHUNKS):
        wait_x(c)
        if c < CHUNKS // 2:
            to_across(c).start()
        to_twin(1, c).start()
        from_source(own_half, 2, c)
        wait_y(c)
        if c >= CHUNKS // 2:
            to_across(c).start()
        to_twin(2, c).start()
        from_source(far_half, 0, c)
        wait_twin(1, c)
        from_source(own_half, 3, c)
        wait_twin(2, c)
        from_source(far_half, 1, c)
        if c > 0:
            side_step(1, c - 1)
            pass_on(*stream[done])
            done += 1
    side_step(1, CHUNKS - 1)
    for c in range(CHUNKS):
        wait_across(c)
        to_twin(3, c).start()
        from_source(far_half, 2, c)
        wait_twin(3, c)
        from_source(far_half, 3, c)
        pass_on(*stream[done])
        done += 1
        convert_cols((mine[1], mine[2], other[1], other[2])[c])
        if c > 0:
            side_step(2, c - 1)
    while done < 2 * CHUNKS:
        pass_on(*stream[done])
        done += 1
    side_step(2, CHUNKS - 1)
    convert_cols(mine[3])
    convert_cols(other[3])
    for a in range(arcs):
        convert_rows(0, a)
    for c in range(CHUNKS):
        side_step(3, c)
        turn_step(c)
        for _ in range(2):
            pass_on(*stream[done])
            done += 1
        if (c + 1) % per_arc == 0:
            convert_rows(1, c // per_arc)
        if c < CHUNKS // 2:
            multiply(0, tiles * 2 * c // CHUNKS, tiles * 2 * (c + 1) // CHUNKS, 0, arcs, False)
        elif c == CHUNKS // 2:
            multiply(1, 0, tiles, 0, arcs // 2, False)
    multiply(1, 0, tiles, arcs // 2, arcs, True)

    for c in range(CHUNKS):
        to_x(c).wait_send()
        to_y(c).wait_send()
        to_across(c).wait_send()
        for j in range(4):
            to_twin(j, c).wait_send()

    for h, i, c in stream:
        q = 2 * h + i
        pl.when(rides_up(q))(lambda: up(rows.at[q, c], q, c).wait_send())
        pl.when(rides_down(q))(lambda: down(rows.at[q, c], q, c).wait_send())
        p = 2 * place(h) + i
        pl.when(onward(h) & goes_up)(lambda: up(rows.at[p, c], p, c).wait_send())
        pl.when(onward(h) & goes_down)(lambda: down(rows.at[p, c], p, c).wait_send())
    for c in range(CHUNKS):
        for t in range(last):
            pl.when(side_on(t))(lambda: side_send(t, c).wait_send())
        for t in range(1, last + 1):
            pl.when(on_side & (level + t <= last))(lambda: give_turn(t, c).wait_send())
        pl.when(turn_on(c))(lambda: turn_send(c).wait_send())


def fused(row_count, planes):
    def body(harmonic, legendre, whitening, longitude, observed):
        arcs, _, width, obs = legendre.shape
        depth = arcs * obs
        tall = row_count * width
        chunk_rows = arcs * width // CHUNKS
        dma = pltpu.SemaphoreType.DMA
        vmem = pl.BlockSpec(memory_space=pltpu.VMEM)
        normal, rhs = pl.pallas_call(
            lambda *refs: kernel(planes, *refs),
            out_shape=(
                jax.ShapeDtypeStruct((planes * width, tall), jnp.float32),
                jax.ShapeDtypeStruct((1, width), jnp.float32),
            ),
            in_specs=[pl.BlockSpec(memory_space=pl.ANY)] * 5,
            out_specs=(vmem, vmem),
            scratch_shapes=[
                pltpu.VMEM((1, width), jnp.int32),
                pltpu.VMEM((arcs, width, obs), jnp.float32),
                pltpu.VMEM((arcs, obs, obs), jnp.float32),
                pltpu.VMEM((arcs, obs), jnp.float32),
                pltpu.VMEM((arcs, obs), jnp.float32),
                pltpu.VMEM((row_count, CHUNKS, chunk_rows, obs), jnp.float32),
                pltpu.VMEM((4, CHUNKS, chunk_rows, obs), jnp.float32),
                pltpu.VMEM((tall, depth), jnp.bfloat16),
                pltpu.VMEM((tall, depth), jnp.bfloat16),
                pltpu.VMEM((2, 2 * width, depth), jnp.bfloat16),
                pltpu.VMEM((2, 2 * width, depth), jnp.bfloat16),
                pltpu.VMEM((planes - 1, CHUNKS, chunk_rows, obs), jnp.float32),
                pltpu.VMEM((CHUNKS, chunk_rows, obs), jnp.float32),
                dma((5,)), dma((CHUNKS,)), dma((CHUNKS,)), dma((CHUNKS,)), dma((4, CHUNKS)),
                dma((4, CHUNKS)), dma((4, CHUNKS)),
                dma((planes - 1, CHUNKS)), dma((planes - 1, CHUNKS)), dma((CHUNKS,)),
                dma((CHUNKS,)), dma((CHUNKS,)), dma((CHUNKS,)), dma((4, CHUNKS)),
                dma((4, CHUNKS)), dma((planes - 1, CHUNKS)), dma((CHUNKS,)),
            ],
            compiler_params=pltpu.CompilerParams(
                collective_id=0, has_side_effects=True, vmem_limit_bytes=56 * 1024 * 1024
            ),
            name="normal_tile",
        )(harmonic, legendre.reshape(arcs, width, obs), whitening, longitude, observed)
        return normal, rhs

    return body


def general(harmonic, legendre, whitening, longitude, observed):
    arcs = legendre.shape[0]
    azimuth = harmonic.reshape(-1)
    leg = legendre.reshape(arcs, -1, legendre.shape[3])
    is_sine = jnp.where(azimuth > LMAX, 1, 0)
    orders = (azimuth - LMAX * is_sine).astype(jnp.float32)
    wave = azimuth_wave(orders[None, :, None], is_sine[None, :, None], longitude[:, None, :])
    high = lax.Precision.HIGH
    portion = jnp.einsum("apo,aqo->apq", leg * wave, whitening, precision=high)
    white_obs = jnp.einsum("aqo,ao->aq", whitening, observed, precision=high)
    rhs = jnp.einsum("apq,aq->p", portion, white_obs, precision=high).reshape(1, -1)
    row_width = portion.shape[1] * lax.axis_size("col")
    groups = lax.axis_size("row") // lax.axis_size("col")
    row_index = lax.axis_index("row")
    column_set = lax.all_gather(portion, "row", axis=1, tiled=True)
    own = lax.dynamic_slice_in_dim(column_set, row_index % groups * row_width, row_width, 1)
    kept = jnp.where(lax.axis_index("col") == row_index // groups, own, 0)
    row_set = lax.psum(kept, "col")
    return jnp.einsum("aio,ajo->ij", row_set, column_set, precision=high), rhs


def solution(mesh):
    in_specs = (P("col", "row"), P(None, "col", "row", None), P(), P(), P())
    out_specs = (P("row", "col"), P("col", "row"))
    row_count, planes = mesh.shape["row"], mesh.shape["col"]
    cube = row_count == 2 ** 3 and row_count == 2 * planes
    body = fused(row_count, planes) if cube else general
    return jax.shard_map(body, mesh=mesh, in_specs=in_specs, out_specs=out_specs, check_vma=False)
```

```python
import jax
import jax.numpy as jnp
from jax import lax
from jax.experimental import pallas as pl
from jax.experimental.pallas import tpu as pltpu
from jax.sharding import PartitionSpec as P

LMAX = 156
CHUNKS = 4
MESH = pl.DeviceIdType.MESH


def azimuth_wave(orders, is_sine, longitude):
    angle = orders * longitude
    turns = jnp.floor(angle * 0.6366197723675814 + 0.5)
    rest = angle - turns * 1.5703125
    rest = rest - turns * 4.837512969970703125e-4
    rest = rest - turns * 7.54978995489188216e-8
    sq = rest * rest
    sine = rest + rest * sq * (-1.6666654611e-1 + sq * (8.3321608736e-3 - 1.9515295891e-4 * sq))
    cosine = 1.0 - 0.5 * sq + sq * sq * (
        4.166664568298827e-2 + sq * (-1.388731625493765e-3 + 2.443315711809948e-5 * sq)
    )
    quarter = turns.astype(jnp.int32) - is_sine
    value = jnp.where((quarter & 1) == 1, sine, cosine)
    return jnp.where(((quarter + 1) & 2) == 2, -value, value)


def split(value):
    high = value.astype(jnp.bfloat16)
    return high, (value - high.astype(jnp.float32)).astype(jnp.bfloat16)


def dot_t(a, b):
    return lax.dot_general(a, b, (((1,), (1,)), ((), ())), preferred_element_type=jnp.float32)


def dot3(a_high, a_low, b_high, b_low):
    return dot_t(a_high, b_low) + dot_t(a_low, b_high) + dot_t(a_high, b_high)


def kernel(
    planes,
    harmonic_in, leg_in, whitening_in, longitude_in, observed_in,
    normal_ref, rhs_ref,
    harmonic_ref, leg_ref, whitening_ref, longitude_ref, observed_ref,
    cols, rows, col_high, col_low, row_high, row_low, side, turn,
    s_in, s_x, s_y, s_d, s_c, s_up, s_dn, s_side, s_give, s_turn,
    r_x, r_y, r_d, r_c, r_z, r_side, r_turn,
):
    fetches = [
        pltpu.make_async_copy(src, dst, s_in.at[n])
        for n, (src, dst) in enumerate((
            (harmonic_in, harmonic_ref), (longitude_in, longitude_ref), (observed_in, observed_ref),
            (leg_in, leg_ref), (whitening_in, whitening_ref),
        ))
    ]
    for fetch in fetches:
        fetch.start()
    arcs, width, obs = leg_ref.shape
    per_arc = CHUNKS // arcs
    me = lax.axis_index("row")
    z = lax.axis_index("col")
    y, x, core = me // 4, (me // 2) % 2, me % 2
    chip = me // 2

    def at(yy, xx, cc):
        return 4 * yy + 2 * xx + cc

    near_x = at(y, 1 - x, core)
    near_y = at(1 - y, x, core)
    across = at(1 - y, 1 - x, core)
    twin = at(y, x, 1 - core)
    mine = (me, near_x, near_y, across)
    other = (twin, at(y, 1 - x, 1 - core), at(1 - y, x, 1 - core), at(1 - y, 1 - x, 1 - core))
    low_z, high_z = jnp.maximum(z - 1, 0), jnp.minimum(z + 1, planes - 1)

    barrier = pltpu.get_barrier_semaphore()
    for peer in (near_x, near_y, twin, other[1], other[2]):
        pl.semaphore_signal(barrier, inc=1, device_id={"row": peer}, device_id_type=MESH)

    @pl.when(z > 0)
    def _():
        pl.semaphore_signal(barrier, inc=1, device_id={"col": low_z}, device_id_type=MESH)

    @pl.when(z < planes - 1)
    def _():
        pl.semaphore_signal(barrier, inc=1, device_id={"col": high_z}, device_id_type=MESH)

    for fetch in fetches:
        fetch.wait()
    code = jnp.transpose(jnp.broadcast_to(harmonic_ref[...], (width, width)))[:, :1]
    is_sine = jnp.where(code > LMAX, 1, 0)
    orders = (code - LMAX * is_sine).astype(jnp.float32)
    rows_per = width // per_arc
    rhs = jnp.zeros((8, width), jnp.float32)
    for a in range(arcs):
        wave = azimuth_wave(orders, is_sine, longitude_ref[a : a + 1, :])
        d_high, d_low = split(leg_ref[a] * wave)
        w_high, w_low = split(whitening_ref[a])
        part = dot3(d_high, d_low, w_high, w_low)
        for i in range(per_arc):
            cols[me, a * per_arc + i] = part[i * rows_per : (i + 1) * rows_per]
        o_high, o_low = split(jnp.broadcast_to(observed_ref[a : a + 1, :], (8, obs)))
        g_high, g_low = split(dot3(o_high, o_low, w_high, w_low))
        p_high, p_low = split(part)
        rhs = rhs + dot3(g_high, g_low, p_high, p_low)
    rhs_ref[...] = rhs[:1]

    inner = jnp.where(z > 0, 1, 0) + jnp.where(z < planes - 1, 1, 0)
    pl.semaphore_wait(barrier, 5 + inner)

    def copy(src, dst, s, r, **device):
        return pltpu.make_async_remote_copy(
            src_ref=src, dst_ref=dst, send_sem=s, recv_sem=r, device_id=device, device_id_type=MESH
        )

    def block(slot, c):
        return cols.at[slot, c]

    def to_x(c):
        return copy(block(me, c), block(me, c), s_x.at[c], r_x.at[c], row=near_x)

    def to_y(c):
        return copy(block(me, c), block(me, c), s_y.at[c], r_y.at[c], row=near_y)

    def to_across(c):
        if c < CHUNKS // 2:
            return copy(block(near_x, c), block(near_x, c), s_d.at[c], r_d.at[c], row=near_y)
        return copy(block(near_y, c), block(near_y, c), s_d.at[c], r_d.at[c], row=near_x)

    def to_twin(j, c):
        return copy(block(mine[j], c), block(mine[j], c), s_c.at[j, c], r_c.at[j, c], row=twin)

    def wait_x(c):
        copy(block(near_x, c), block(near_x, c), s_x.at[c], r_x.at[c], row=near_x).wait_recv()

    def wait_y(c):
        copy(block(near_y, c), block(near_y, c), s_y.at[c], r_y.at[c], row=near_y).wait_recv()

    def wait_across(c):
        copy(block(across, c), block(across, c), s_d.at[c], r_d.at[c], row=near_x).wait_recv()

    def wait_twin(j, c):
        copy(block(other[j], c), block(other[j], c), s_c.at[j, c], r_c.at[j, c], row=twin).wait_recv()

    source = z == chip
    own_half = y == core
    goes_up = (z >= chip) & (z < planes - 1)
    goes_down = (z <= chip) & (z > 0)
    far_y = y + core - 2 * y * core
    line_y = y + far_y - 2 * y * far_y

    def line_slot(q):
        xx = x if q < 2 else 1 - x
        cc = core if q % 2 == 0 else 1 - core
        return at(line_y, xx, cc)

    last = planes - 1
    by_side = ((z < chip) & (core == 0)) | ((z > chip) & (core == 1))
    side_x = jnp.where(core == 0, 0, 1)
    swap = jnp.where(by_side & (x == side_x), 1, 0)

    def up(src, q, c):
        return copy(src, rows.at[q, c], s_up.at[q, c], r_z.at[q, c], col=high_z)

    def down(src, q, c):
        return copy(src, rows.at[q, c], s_dn.at[q, c], r_z.at[q, c], col=low_z)

    def rides_up(q):
        has_side_x = (x == side_x) if q < 2 else (x != side_x)
        return source & goes_up & jnp.logical_not(has_side_x & (core == 1))

    def rides_down(q):
        has_side_x = (x == side_x) if q < 2 else (x != side_x)
        return source & goes_down & jnp.logical_not(has_side_x & (core == 0))

    def from_source(condition, q, c):
        @pl.when(condition & rides_up(q))
        def _():
            up(block(line_slot(q), c), q, c).start()

        @pl.when(condition & rides_down(q))
        def _():
            down(block(line_slot(q), c), q, c).start()

    relay = jnp.logical_not(source)

    def place(h):
        return h + swap - 2 * h * swap

    def onward(h):
        return relay if h == 0 else relay & jnp.logical_not(by_side)

    def pass_on(h, i, c):
        q = 2 * place(h) + i

        @pl.when(relay)
        def _():
            up(rows.at[q, c], q, c).wait_recv()

        @pl.when(onward(h) & goes_up)
        def _():
            up(rows.at[q, c], q, c).start()

        @pl.when(onward(h) & goes_down)
        def _():
            down(rows.at[q, c], q, c).start()

    on_side = (chip == 0) | (chip == last)
    level = jnp.where(chip == last, last - z, z)
    further = jnp.where(chip == 0, low_z, high_z)

    def side_send(t, c):
        src = block(me, c) if t == 0 else side.at[t - 1, c]
        return copy(src, side.at[t, c], s_side.at[t, c], r_side.at[t, c], col=further)

    def side_on(t):
        held = on_side & (level > 0)
        return held if t == 0 else held & (level + t <= last)

    def give_x(t, c):
        q = 2 + far_y
        return copy(side.at[t - 1, c], rows.at[q, c], s_give.at[t - 1, c], r_z.at[q, c], row=at(y, 1 - x, y))

    def give_y(t, c):
        q = far_y
        return copy(side.at[t - 1, c], rows.at[q, c], s_give.at[t - 1, c], r_z.at[q, c], row=at(1 - y, x, y))

    def give_turn(t, c):
        peer = near_x if c < CHUNKS // 2 else near_y
        return copy(side.at[t - 1, c], turn.at[c], s_give.at[t - 1, c], r_turn.at[c], row=peer)

    gives = ((1, give_x), (2, give_y), (3, give_turn))

    def side_step(t, c):
        @pl.when(on_side & (level + t <= last))
        def _():
            side_send(t - 1, c).wait_recv()
            if t < last:
                @pl.when(level > 0)
                def _():
                    side_send(t, c).start()
            for k, give in gives:
                if k >= t:
                    @pl.when(level + t == k)
                    def _():
                        give(t, c).start()

    def turn_on(c):
        from_low = (x == 1) if c < CHUNKS // 2 else (x == 0)
        there = (from_low & (z < last)) | (jnp.logical_not(from_low) & (z > 0))
        return jnp.logical_not(on_side) & there

    def turn_send(c):
        if c < CHUNKS // 2:
            q, peer = 2 + far_y, at(1 - y, x, y)
        else:
            q, peer = 3 - far_y, at(y, 1 - x, 1 - y)
        return copy(turn.at[c], rows.at[q, c], s_turn.at[c], r_z.at[q, c], row=peer)

    def turn_step(c):
        @pl.when(turn_on(c))
        def _():
            copy(turn.at[c], turn.at[c], s_turn.at[c], r_turn.at[c], row=near_x).wait_recv()
            turn_send(c).start()

    far_half = jnp.logical_not(own_half)
    stream = [(h, i, c) for h in range(2) for c in range(CHUNKS) for i in range(2)]
    per_tile = width * 2
    tiles = col_high.shape[0] // per_tile

    def convert_cols(slot):
        for c in range(CHUNKS):
            a, i = c // per_arc, c % per_arc
            high, low = split(cols[slot, c])
            start = pl.multiple_of(slot * width + i * rows_per, rows_per)
            col_high[pl.ds(start, rows_per), pl.ds(a * obs, obs)] = high
            col_low[pl.ds(start, rows_per), pl.ds(a * obs, obs)] = low

    def convert_rows(h, a):
        def put(i, c, value):
            high, low = split(value)
            cc = core if i == 0 else 1 - core
            start = pl.multiple_of(cc * width + (c % per_arc) * rows_per, rows_per)
            row_high[h, pl.ds(start, rows_per), pl.ds(a * obs, obs)] = high
            row_low[h, pl.ds(start, rows_per), pl.ds(a * obs, obs)] = low

        for i in range(2):
            for c in range(a * per_arc, (a + 1) * per_arc):
                @pl.when(source)
                def _():
                    put(i, c, cols[line_slot(2 * h + i), c])

                @pl.when(relay)
                def _():
                    put(i, c, rows[2 * place(h) + i, c])

    def multiply(h, start, stop, low_a, high_a, add):
        turned = place(h)
        xx = x + turned - 2 * x * turned
        top = pl.multiple_of(xx * per_tile, per_tile)
        depth = slice(low_a * obs, high_a * obs)

        def one(j, carry):
            left = pl.multiple_of(j * per_tile, per_tile)
            tile = (pl.ds(top, per_tile), pl.ds(left, per_tile))
            part = dot3(
                row_high[h, :, depth], row_low[h, :, depth],
                col_high[pl.ds(left, per_tile), depth], col_low[pl.ds(left, per_tile), depth],
            )
            normal_ref[tile] = normal_ref[tile] + part if add else part
            return carry

        lax.fori_loop(start, stop, one, 0)

    for c in range(CHUNKS):
        @pl.when(side_on(0))
        def _():
            side_send(0, c).start()

        to_x(c).start()
        to_y(c).start()
        to_twin(0, c).start()
        from_source(own_half, 0, c)
    for c in range(CHUNKS):
        wait_twin(0, c)
        from_source(own_half, 1, c)
    convert_cols(me)
    convert_cols(twin)
    done = 0
    for c in range(CHUNKS):
        wait_x(c)
        if c < CHUNKS // 2:
            to_across(c).start()
        to_twin(1, c).start()
        from_source(own_half, 2, c)
        wait_y(c)
        if c >= CHUNKS // 2:
            to_across(c).start()
        to_twin(2, c).start()
        from_source(far_half, 0, c)
        wait_twin(1, c)
        from_source(own_half, 3, c)
        wait_twin(2, c)
        from_source(far_half, 1, c)
        if c > 0:
            side_step(1, c - 1)
            pass_on(*stream[done])
            done += 1
    side_step(1, CHUNKS - 1)
    for c in range(CHUNKS):
        wait_across(c)
        to_twin(3, c).start()
        from_source(far_half, 2, c)
        wait_twin(3, c)
        from_source(far_half, 3, c)
        pass_on(*stream[done])
        done += 1
        convert_cols((mine[1], mine[2], other[1], other[2])[c])
        if c > 0:
            side_step(2, c - 1)
    while done < 2 * CHUNKS:
        pass_on(*stream[done])
        done += 1
    side_step(2, CHUNKS - 1)
    convert_cols(mine[3])
    convert_cols(other[3])
    for a in range(arcs):
        convert_rows(0, a)
    for c in range(CHUNKS):
        side_step(3, c)
        for _ in range(2):
            pass_on(*stream[done])
            done += 1
        turn_step(c)
        if (c + 1) % per_arc == 0:
            convert_rows(1, c // per_arc)
        if c < CHUNKS // 2:
            multiply(0, tiles * 2 * c // CHUNKS, tiles * 2 * (c + 1) // CHUNKS, 0, arcs, False)
        elif c == CHUNKS // 2:
            multiply(1, 0, tiles, 0, arcs // 2, False)
    multiply(1, 0, tiles, arcs // 2, arcs, True)

    for c in range(CHUNKS):
        to_x(c).wait_send()
        to_y(c).wait_send()
        to_across(c).wait_send()
        for j in range(4):
            to_twin(j, c).wait_send()

    for h, i, c in stream:
        q = 2 * h + i
        pl.when(rides_up(q))(lambda: up(rows.at[q, c], q, c).wait_send())
        pl.when(rides_down(q))(lambda: down(rows.at[q, c], q, c).wait_send())
        p = 2 * place(h) + i
        pl.when(onward(h) & goes_up)(lambda: up(rows.at[p, c], p, c).wait_send())
        pl.when(onward(h) & goes_down)(lambda: down(rows.at[p, c], p, c).wait_send())
    for c in range(CHUNKS):
        for t in range(last):
            pl.when(side_on(t))(lambda: side_send(t, c).wait_send())
        for t in range(1, last + 1):
            pl.when(on_side & (level + t <= last))(lambda: give_turn(t, c).wait_send())
        pl.when(turn_on(c))(lambda: turn_send(c).wait_send())


def fused(row_count, planes):
    def body(harmonic, legendre, whitening, longitude, observed):
        arcs, _, width, obs = legendre.shape
        depth = arcs * obs
        tall = row_count * width
        chunk_rows = arcs * width // CHUNKS
        dma = pltpu.SemaphoreType.DMA
        vmem = pl.BlockSpec(memory_space=pltpu.VMEM)
        normal, rhs = pl.pallas_call(
            lambda *refs: kernel(planes, *refs),
            out_shape=(
                jax.ShapeDtypeStruct((planes * width, tall), jnp.float32),
                jax.ShapeDtypeStruct((1, width), jnp.float32),
            ),
            in_specs=[pl.BlockSpec(memory_space=pl.ANY)] * 5,
            out_specs=(vmem, vmem),
            scratch_shapes=[
                pltpu.VMEM((1, width), jnp.int32),
                pltpu.VMEM((arcs, width, obs), jnp.float32),
                pltpu.VMEM((arcs, obs, obs), jnp.float32),
                pltpu.VMEM((arcs, obs), jnp.float32),
                pltpu.VMEM((arcs, obs), jnp.float32),
                pltpu.VMEM((row_count, CHUNKS, chunk_rows, obs), jnp.float32),
                pltpu.VMEM((4, CHUNKS, chunk_rows, obs), jnp.float32),
                pltpu.VMEM((tall, depth), jnp.bfloat16),
                pltpu.VMEM((tall, depth), jnp.bfloat16),
                pltpu.VMEM((2, 2 * width, depth), jnp.bfloat16),
                pltpu.VMEM((2, 2 * width, depth), jnp.bfloat16),
                pltpu.VMEM((planes - 1, CHUNKS, chunk_rows, obs), jnp.float32),
                pltpu.VMEM((CHUNKS, chunk_rows, obs), jnp.float32),
                dma((5,)), dma((CHUNKS,)), dma((CHUNKS,)), dma((CHUNKS,)), dma((4, CHUNKS)),
                dma((4, CHUNKS)), dma((4, CHUNKS)),
                dma((planes - 1, CHUNKS)), dma((planes - 1, CHUNKS)), dma((CHUNKS,)),
                dma((CHUNKS,)), dma((CHUNKS,)), dma((CHUNKS,)), dma((4, CHUNKS)),
                dma((4, CHUNKS)), dma((planes - 1, CHUNKS)), dma((CHUNKS,)),
            ],
            compiler_params=pltpu.CompilerParams(
                collective_id=0, has_side_effects=True, vmem_limit_bytes=56 * 1024 * 1024
            ),
            name="normal_tile",
        )(harmonic, legendre.reshape(arcs, width, obs), whitening, longitude, observed)
        return normal, rhs

    return body


def general(harmonic, legendre, whitening, longitude, observed):
    arcs = legendre.shape[0]
    azimuth = harmonic.reshape(-1)
    leg = legendre.reshape(arcs, -1, legendre.shape[3])
    is_sine = jnp.where(azimuth > LMAX, 1, 0)
    orders = (azimuth - LMAX * is_sine).astype(jnp.float32)
    wave = azimuth_wave(orders[None, :, None], is_sine[None, :, None], longitude[:, None, :])
    high = lax.Precision.HIGH
    portion = jnp.einsum("apo,aqo->apq", leg * wave, whitening, precision=high)
    white_obs = jnp.einsum("aqo,ao->aq", whitening, observed, precision=high)
    rhs = jnp.einsum("apq,aq->p", portion, white_obs, precision=high).reshape(1, -1)
    row_width = portion.shape[1] * lax.axis_size("col")
    groups = lax.axis_size("row") // lax.axis_size("col")
    row_index = lax.axis_index("row")
    column_set = lax.all_gather(portion, "row", axis=1, tiled=True)
    own = lax.dynamic_slice_in_dim(column_set, row_index % groups * row_width, row_width, 1)
    kept = jnp.where(lax.axis_index("col") == row_index // groups, own, 0)
    row_set = lax.psum(kept, "col")
    return jnp.einsum("aio,ajo->ij", row_set, column_set, precision=high), rhs


def solution(mesh):
    in_specs = (P("col", "row"), P(None, "col", "row", None), P(), P(), P())
    out_specs = (P("row", "col"), P("col", "row"))
    row_count, planes = mesh.shape["row"], mesh.shape["col"]
    cube = row_count == 2 ** 3 and row_count == 2 * planes
    body = fused(row_count, planes) if cube else general
    return jax.shard_map(body, mesh=mesh, in_specs=in_specs, out_specs=out_specs, check_vma=False)
```
